32 devices in a mesh: rep: 2 (over x), grp: 8 (over z, y), loc: 2 (over core).
Axes of the slice: x: 2, y: 2, z: 4, core: 2. Of those that a mesh axis runs over, the one named last changes fastest.
Arguments:
- moe_tokens: bfloat16 [128, 7168], P(('rep', 'grp', 'loc')), parts along dimension 0, may hold values from -6 to 6
- picked_groups: int32 [128, 4], P(('rep', 'grp', 'loc')), parts along dimension 0, may hold values from 0 to 7, all different within a row; in each aligned block of 4 rows (0 to 3, 4 to 7, ...) at most 3 rows name the same one
- gate_scores: float32 [128, 4], P(('rep', 'grp', 'loc')), parts along dimension 0, may hold values from 0.2 to 1.2
- w_gate: bfloat16 [8, 7168, 2048], P('grp', None, 'loc'), may hold values from -0.0625 to 0.0625
- w_up: bfloat16 [8, 7168, 2048], P('grp', None, 'loc'), may hold values from -0.0625 to 0.0625
- w_down: bfloat16 [8, 2048, 7168], P('grp', 'loc'), may hold values from -0.125 to 0.125
- query_latent: bfloat16 [64, 128, 512], P(('rep', 'grp', 'loc')), parts along dimension 0, may hold values from -9 to 9
- query_rope: bfloat16 [64, 8192], P(('rep', 'grp', 'loc')), parts along dimension 0, may hold values from -9 to 93
- cache_latent: bfloat16 [64, 2048, 512], P(('rep', 'grp', 'loc')), parts along dimension 0, may hold values from -6 to 6
- cache_rope: bfloat16 [64, 64, 2048], P(('rep', 'grp', 'loc')), parts along dimension 0, may hold values from -6 to 6
- cache_lengths: int32 [64], P(('rep', 'grp', 'loc')), parts along dimension 0, may hold values from 256 to 2048, as said below
Outputs:
- moe_out: bfloat16 [128, 7168], P(('rep', 'grp', 'loc')), parts along dimension 0
- attn_out: bfloat16 [64, 128, 512], P(('rep', 'grp', 'loc')), parts along dimension 0
The draws below stay inside these ranges and needn't reach their ends.
There are 2 independent parts, one for each index of `rep`. The reference program is written for one: setup_inputs(seed, part) draws one part's arguments, and reference() takes and returns one part's arrays. A program takes and returns all parts, laid end to end along the dimension named above; an argument that names none is the same for every part. Nothing has to cross between parts.
Inputs may be any that keep to these rules, and one draw needn't show every extreme that they name: `picked_groups`: the 4 groups of a token differ; at most 3 of the 4 tokens of one device pick the same group, and in every draw some device has exactly 3 tokens for some group. `cache_lengths`: in every draw some request has all 2048 positions.
All inputs are finite; a program needn't handle non-finite values.
Results may differ from the reference program's by a relative error of at most 0.0066.
Values may be sent and summed in bfloat16 or wider, within the bound.
A program may use at most 128 MiB of HBM per device.

```python
import math
import jax
import jax.numpy as jnp
import numpy as np
from jax import lax

D = 7168
H = 2048
HEADS = 128
LATENT = 512
ROPE = 64
PICKS = 4
TOK_DEV = 4
LEN = 2048
TOKENS = 64
REQS = 32
MOST = 3
N_GRP = 8
N_LOC = 2


def draw_query_latent(key, part):
    key = jax.random.fold_in(key, 7)
    values = jnp.clip(1.5 * jax.random.normal(key, (REQS, HEADS, LATENT), jnp.float32), -9.0, 9.0)
    return values.astype(jnp.bfloat16)


def draw_query_rope(key, part):
    key = jax.random.fold_in(key, 13)
    values = jnp.clip(1.5 * jax.random.normal(key, (REQS, HEADS, ROPE), jnp.float32), -9.0, 9.0)
    return values.reshape(REQS, HEADS * ROPE).astype(jnp.bfloat16)


def draw_cache_rope(key, part):
    key = jax.random.fold_in(key, 19)
    values = jnp.clip(jax.random.normal(key, (REQS, ROPE, LEN), jnp.float32), -6.0, 6.0)
    return values.astype(jnp.bfloat16)


def draw_cache_lengths(key, part):
    key = jax.random.fold_in(key, 23)
    length_key, full_key = jax.random.split(key)
    lengths = jax.random.randint(length_key, (REQS,), LEN // 8, LEN + 1, jnp.int32)
    full_index = jax.random.randint(full_key, (), 0, REQS, jnp.int32)
    return jnp.where(jnp.arange(REQS) == full_index, LEN, lengths).astype(jnp.int32)


def block_levels(rng, shape, shards, low, high):
    level = 1.0
    for dim, parts in shards:
        heights = jax.random.uniform(jax.random.fold_in(jax.random.fold_in(rng, 6), dim), (parts,), jnp.float32, low / len(shards), high / len(shards))
        level = level * jnp.repeat(jnp.exp(heights), shape[dim] // parts).reshape((-1,) + (1,) * (len(shape) - 1 - dim))
    return level


def routed_block(key, own, number, rows, count, top, limit, lean):
    sequence = jax.random.permutation(key, count)
    packed, ordinary = shares(count, rows * top, limit, lean, True), shares(count, rows * top, limit, lean, False)
    places = jnp.arange(count)

    def named(tallies, turn):
        used = int((tallies > 0).sum())
        fixed = max(1, used // 4)
        shifted = fixed + (places - fixed + turn * (used - fixed)) % max(1, count - fixed)
        return jnp.zeros((count,), jnp.int32).at[sequence[jnp.where(places < fixed, places, shifted)]].set(jnp.asarray(tallies, jnp.int32))

    tallies = jnp.where(number % 4 == 0, named(packed, number // 4), named(ordinary, number - number // 4 - 1))
    mixed = jax.random.permutation(jax.random.fold_in(own, 3), count)
    source_of, taker = mixed[0:count // 2 * 2:2], mixed[1:count // 2 * 2:2]
    margin = jnp.minimum(tallies[source_of] - 1, limit - tallies[taker]) // 2
    margin = jnp.where((source_of == sequence[0]) | (taker == sequence[0]) | (tallies[taker] == 0), 0, jnp.maximum(margin, 0))
    shifted = jax.random.randint(jax.random.fold_in(own, 4), (count // 2,), 0, 1 << 20) % (margin + 1)
    tallies = tallies.at[source_of].add(-shifted).at[taker].add(shifted)
    labels = jnp.searchsorted(jnp.cumsum(tallies), jnp.arange(rows * top), side="right").astype(jnp.int32)
    listing = labels.reshape(top, rows).T
    listing = listing[jax.random.permutation(jax.random.fold_in(own, 1), rows)]
    turn = jax.random.randint(jax.random.fold_in(own, 2), (rows, 1), 0, top)
    return jnp.take_along_axis(listing, (jnp.arange(top)[None, :] + turn) % top, axis=1)


def shares(count, total, most, slope, full):
    loads = [(1 << 20) // math.isqrt(grade ** slope) + 1 for grade in range(1, count + 1)]
    largest = most if full else min(most, max(-(-total // count), total * loads[0] // sum(loads)))
    least = 1 if total - largest >= count - 1 else 0
    counts, spare = [largest] + [least] * (count - 1), total - largest - least * (count - 1)
    while spare > 0:
        free = [i for i in range(1, count) if counts[i] < largest] or [i for i in range(1, count) if counts[i] < most]
        pool, budget = sum([loads[i] for i in free]), spare
        for i in free:
            extra = min(most - counts[i], max(1, budget * loads[i] // pool), spare)
            counts[i] = counts[i] + extra
            spare = spare - extra
    return np.array(counts)


def normal_values(rng, dims, spread, reach, cuts=(), kind=jnp.bfloat16):
    result = spread * jax.random.normal(rng, dims, jnp.float32)
    if cuts:
        result = result * block_levels(rng, dims, cuts, -0.22, 0.18)
    return jnp.clip(result, -reach, reach).astype(kind)


def setup_inputs(seed: int = 0, part: int = 0) -> dict:
    key_list = jax.random.split(jax.random.key(seed), 12)
    part_splits = jax.random.split(jax.random.fold_in(key_list[11], part), 12)
    moe_tokens = normal_values(part_splits[0], (TOKENS, D), 1.0, 6.0, ((0, 16),))
    picked_groups_keys = jax.random.split(jax.random.fold_in(part_splits[1], 1), TOKENS // TOK_DEV)
    picked_groups_turns = jax.random.permutation(jax.random.fold_in(part_splits[1], 3), TOKENS // TOK_DEV)
    picked_groups = jax.vmap(lambda own, number: routed_block(jax.random.fold_in(part_splits[1], 2), own, number, TOK_DEV, N_GRP, PICKS, MOST, 2))(picked_groups_keys, picked_groups_turns).reshape((TOKENS, PICKS))
    gate_scores = jnp.clip(0.2 + 1 * jax.random.uniform(part_splits[2], (TOKENS, PICKS), jnp.float32) ** block_levels(part_splits[2], (TOKENS, PICKS), ((0, 16),), -0.2, 0.2), 0.2, 1.2)
    w_gate = normal_values(key_list[3], (N_GRP, D, H), D ** -0.5, 0.0625, ((0, 8), (2, 2)))
    w_up = normal_values(key_list[4], (N_GRP, D, H), D ** -0.5, 0.0625, ((0, 8), (2, 2)))
    w_down = normal_values(key_list[5], (N_GRP, H, D), H ** -0.5, 0.125, ((0, 8), (1, 2)))
    query_latent = draw_query_latent(jax.random.fold_in(jax.random.fold_in(key_list[11], part), 71), part)
    query_rope = draw_query_rope(jax.random.fold_in(jax.random.fold_in(key_list[11], part), 71), part)
    cache_latent = normal_values(part_splits[8], (REQS, LEN, LATENT), 1.0, 6.0, ((0, 16),))
    cache_rope = draw_cache_rope(jax.random.fold_in(jax.random.fold_in(key_list[11], part), 71), part)
    cache_lengths = draw_cache_lengths(jax.random.fold_in(jax.random.fold_in(key_list[11], part), 71), part)
    return dict(moe_tokens=moe_tokens, picked_groups=picked_groups, gate_scores=gate_scores, w_gate=w_gate, w_up=w_up, w_down=w_down, query_latent=query_latent, query_rope=query_rope, cache_latent=cache_latent, cache_rope=cache_rope, cache_lengths=cache_lengths)


softmax_scale = 192.0 ** -0.5
mask_fill = -1.0e30


def expert_output(tokens, gate_matrix, up_matrix, down_matrix):
    gate_pre = jnp.dot(tokens, gate_matrix, preferred_element_type=jnp.float32)
    up_pre = jnp.dot(tokens, up_matrix, preferred_element_type=jnp.float32)
    hidden_act = (jax.nn.silu(gate_pre) * up_pre).astype(jnp.bfloat16)
    block_width = H // N_LOC
    hidden_blocks = hidden_act.reshape(tokens.shape[0], N_LOC, block_width).transpose(1, 0, 2)
    down_blocks = down_matrix.reshape(N_LOC, block_width, down_matrix.shape[1])

    def add_block(running, block_pair):
        hidden_block, down_block = block_pair
        block_term = jnp.dot(hidden_block, down_block, preferred_element_type=jnp.float32).astype(jnp.bfloat16)
        block_term = lax.optimization_barrier(block_term)
        return running + block_term.astype(jnp.float32), None

    start_sum = jnp.zeros((tokens.shape[0], down_matrix.shape[1]), jnp.float32)
    summed = lax.scan(add_block, start_sum, (hidden_blocks, down_blocks))[0]
    return summed.astype(jnp.bfloat16)


def attend(inputs):
    query_block, rotary_block, cache_block, rotary_keys, length_now = inputs
    scores = jnp.dot(query_block, cache_block.T, preferred_element_type=jnp.float32)
    scores = scores + jnp.dot(rotary_block.reshape(HEADS, ROPE), rotary_keys, preferred_element_type=jnp.float32)
    scores = scores * softmax_scale
    positions = jnp.arange(LEN, dtype=jnp.int32)
    scores = jnp.where(positions[None, :] < length_now, scores, mask_fill)
    row_max = jnp.max(scores, axis=1, keepdims=True)
    exp_scores = jnp.exp(scores - row_max)
    weights = (exp_scores / jnp.sum(exp_scores, axis=1, keepdims=True)).astype(jnp.bfloat16)
    return jnp.dot(weights, cache_block, preferred_element_type=jnp.float32).astype(jnp.bfloat16)


def reference(moe_tokens, picked_groups, gate_scores, w_gate, w_up, w_down, query_latent, query_rope, cache_latent, cache_rope, cache_lengths):
    group_ids = jnp.arange(N_GRP, dtype=jnp.int32)

    def add_group(running, inputs):
        group_index, gate_matrix, up_matrix, down_matrix = inputs
        expert_out = expert_output(moe_tokens, gate_matrix, up_matrix, down_matrix)
        weight = jnp.sum(jnp.where(picked_groups == group_index, gate_scores, jnp.zeros_like(gate_scores)), axis=1)
        return running + weight[:, None] * expert_out.astype(jnp.float32), None

    start_out = jnp.zeros((moe_tokens.shape[0], moe_tokens.shape[1]), jnp.float32)
    mixed_sum = lax.scan(add_group, start_out, (group_ids, w_gate, w_up, w_down))[0]
    moe_out = mixed_sum.astype(jnp.bfloat16)
    attn_out = lax.map(attend, (query_latent, query_rope, cache_latent, cache_rope, cache_lengths))
    return (moe_out, attn_out)
```

```python
import functools
import jax
import jax.numpy as jnp
from jax import lax
from jax.experimental import pallas as pl
from jax.experimental.pallas import tpu as pltpu
from jax.sharding import PartitionSpec as P

softmax_scale = 192.0 ** (-0.5)
mask_fill = -1e30
MESH = pl.DeviceIdType.MESH
EXT = 128
F32 = jnp.float32
BF16 = jnp.bfloat16


def fused(cfg, *refs):
    ng, nl, no, nh, kc, nc, pc = cfg
    (tok, picks, gsc, lens, qlat, qrope, wg_h, wu_h, wd_h, cl_h, cr_h,
     moe_out, attn_out,
     wg, wu, wd, cl, cr, sc, gat, x32, accg, accu, hs,
     sb1, rb1, sb2, rb2, sb3, rb3,
     wsem, dsem, csem, ghs, ghr, gos, gor, gls, glr,
     s1s, s1r, s2s, s2r, s3s, s3r) = refs
    tk, d = tok.shape
    hl = wg.shape[1]
    reqs, heads, lat = qlat.shape
    length = cl.shape[1]
    g = lax.axis_index("grp")
    l = lax.axis_index("loc")
    hi = g // no
    lo = g % no
    kstep = d // kc
    cw = d // nc

    cache_copies = []
    for r in range(reqs):
        pair = [pltpu.make_async_copy(cl_h.at[r], cl.at[r], csem.at[2 * r]),
                pltpu.make_async_copy(cr_h.at[r], cr.at[r], csem.at[2 * r + 1])]
        for c in pair:
            c.start()
        cache_copies.append(pair)
    w_copies = []
    for k in range(kc):
        rows = pl.ds(k * kstep, kstep)
        pair = [pltpu.make_async_copy(wg_h.at[0, rows], wg.at[rows], wsem.at[2 * k]),
                pltpu.make_async_copy(wu_h.at[0, rows], wu.at[rows], wsem.at[2 * k + 1])]
        for c in pair:
            c.start()
        w_copies.append(pair)
    d_copies = []
    for j in range(nc):
        cols = pl.ds(j * cw, cw)
        c = pltpu.make_async_copy(wd_h.at[0, :, cols], wd.at[:, cols], dsem.at[j])
        c.start()
        d_copies.append(c)

    def hi_dev(k):
        h2 = lax.rem(hi + k, nh)
        return h2, {"grp": h2 * no + lo, "loc": l}

    def lo_dev(k):
        o2 = lax.rem(lo + k, no)
        return o2, {"grp": hi * no + o2, "loc": l}

    def loc_dev(k):
        l2 = lax.rem(l + k, nl)
        return l2, {"grp": g, "loc": l2}

    lane = lax.broadcasted_iota(jnp.int32, (tk, EXT), 1)
    lane_g = lax.rem(lane, ng)
    weight = jnp.zeros((tk, EXT), F32)
    for k in range(picks.shape[1]):
        weight = weight + jnp.where(picks[:, k:k + 1] == lane_g, gsc[:, k:k + 1], 0.0)
    w1 = weight.astype(BF16).astype(F32)
    w2 = (weight - w1).astype(BF16).astype(F32)
    w3 = weight - w1 - w2
    terms = jnp.where(lane < ng, w1, jnp.where(lane < 2 * ng, w2, jnp.where(lane < 3 * ng, w3, 0.0)))
    gat[l, lo, hi, :, 0:d] = tok[...]
    gat[l, lo, hi, :, d:d + EXT] = terms.astype(BF16)

    barrier = pltpu.get_barrier_semaphore()
    peers = [hi_dev(k)[1] for k in range(1, nh)] + [lo_dev(k)[1] for k in range(1, no)] + [
        loc_dev(k)[1] for k in range(1, nl)]
    for dev in peers:
        pl.semaphore_signal(barrier, inc=1, device_id=dev, device_id_type=MESH)
    pl.semaphore_wait(barrier, len(peers))

    def remote(src, dst, ss, rs, dev):
        return pltpu.make_async_remote_copy(
            src_ref=src, dst_ref=dst, send_sem=ss, recv_sem=rs, device_id=dev, device_id_type=MESH)

    g_sends = []

    def go(copy):
        copy.start()
        g_sends.append(copy)

    mine = gat.at[l, lo, hi]
    for k in range(1, nh):
        go(remote(mine, mine, ghs.at[k], ghr.at[k], hi_dev(k)[1]))

    def forward(k):
        h2 = lax.rem(hi - k + nh, nh)
        blk = gat.at[l, lo, h2]
        if k > 0:
            remote(blk, blk, ghs.at[k], ghr.at[k], hi_dev(k)[1]).wait_recv()
        for m in range(1, no):
            go(remote(blk, blk, gos.at[m, k], gor.at[m, k], lo_dev(m)[1]))

    def loc_send(m):
        o2 = lax.rem(lo - m + no, no)
        if m > 0:
            for k in range(nh):
                blk = gat.at[l, o2, lax.rem(hi - k + nh, nh)]
                remote(blk, blk, gos.at[m, k], gor.at[m, k], lo_dev(m)[1]).wait_recv()
        part = gat.at[l, o2]
        for q in range(1, nl):
            go(remote(part, part, gls.at[q, m], glr.at[q, m], loc_dev(q)[1]))

    def loc_wait(m):
        o2 = lax.rem(lo - m + no, no)
        for q in range(1, nl):
            part = gat.at[lax.rem(l - q + nl, nl), o2]
            remote(part, part, gls.at[q, m], glr.at[q, m], loc_dev(q)[1]).wait_recv()

    forward(0)

    pw = length // pc

    def scores_of(r):
        for c in cache_copies[r]:
            c.wait()
        q = qlat[r]
        qr = qrope[r]
        top = None
        for b in range(pc):
            s = lax.dot_general(q, cl[r, b * pw:(b + 1) * pw, :], (((1,), (1,)), ((), ())),
                                preferred_element_type=F32)
            s = s + jnp.dot(qr, cr[r, :, b * pw:(b + 1) * pw], preferred_element_type=F32)
            pos = lax.broadcasted_iota(jnp.int32, (heads, pw), 1) + b * pw
            s = jnp.where(pos < lens[r], s * softmax_scale, mask_fill)
            sc[:, b * pw:(b + 1) * pw] = s
            t = jnp.max(s, axis=1, keepdims=True)
            top = t if top is None else jnp.maximum(top, t)
        return top

    def values_of(r, top):
        acc = jnp.zeros((heads, lat), F32)
        total = jnp.zeros((heads, 1), F32)
        for b in range(pc):
            p = jnp.exp(sc[:, b * pw:(b + 1) * pw] - top)
            total = total + jnp.sum(p, axis=1, keepdims=True)
            acc = acc + jnp.dot(p.astype(BF16), cl[r, b * pw:(b + 1) * pw, :],
                                preferred_element_type=F32)
        attn_out[r] = (acc / total).astype(BF16)

    units = []
    for r in range(reqs):
        box = {}
        units.append(lambda r=r, box=box: box.update(top=scores_of(r)))
        units.append(lambda r=r, box=box: values_of(r, box["top"]))
    steps = [functools.partial(forward, k) for k in range(1, nh)]
    steps.append(functools.partial(loc_send, 0))
    steps += [functools.partial(loc_send, m) for m in range(1, no)]
    order = [[] for _ in units]
    for i, s in enumerate(steps):
        order[min(i, len(units) - 1)].append(s)
    for unit, after in zip(units, order):
        unit()
        for s in after:
            s()
    for m in range(no):
        loc_wait(m)

    per = no * nh

    pack = max(1, 8 // tk)

    def put(i, _):
        parts = []
        for u in range(pack):
            at = i * pack + u
            rest = at % per
            parts.append(gat[at // per, rest // nh, rest % nh].astype(F32))
        x32[pl.ds(pl.multiple_of(i * (pack * tk), 8), pack * tk), :] = jnp.concatenate(parts, axis=0)
        return 0

    packs = nl * per // pack
    lax.fori_loop(0, packs, put, 0, unroll=min(8, packs))

    nt = min(256, hl)
    for k in range(kc):
        for c in w_copies[k]:
            c.wait()
        xk = x32[:, k * kstep:(k + 1) * kstep].astype(BF16)
        for n in range(hl // nt):
            cols = slice(n * nt, (n + 1) * nt)
            rows = slice(k * kstep, (k + 1) * kstep)
            pg = jnp.dot(xk, wg[rows, cols], preferred_element_type=F32)
            pu = jnp.dot(xk, wu[rows, cols], preferred_element_type=F32)
            if k > 0:
                pg = accg[:, cols] + pg
                pu = accu[:, cols] + pu
            if k < kc - 1:
                accg[:, cols] = pg
                accu[:, cols] = pu
            else:
                hs[:, cols] = (pg / (1.0 + jnp.exp(-pg)) * pu).astype(BF16)

    wlane = lax.broadcasted_iota(jnp.int32, (x32.shape[0], EXT), 1)
    hit = (lax.rem(wlane, ng) == g) & (wlane < 3 * ng)
    wcol = jnp.sum(jnp.where(hit, x32[:, d:d + EXT], 0.0), axis=1, keepdims=True)

    out_sends = []

    def send(copy):
        copy.start()
        out_sends.append(copy)

    def stage_m(j):
        d_copies[j].wait()
        y = jnp.dot(hs[...], wd[:, j * cw:(j + 1) * cw], preferred_element_type=F32) * wcol
        for i in range(nl * per):
            rest = i % per
            sb1[j, i // per, rest // nh, rest % nh] = y[i * tk:(i + 1) * tk].astype(BF16)
        for q in range(1, nl):
            l2, dev = loc_dev(q)
            send(remote(sb1.at[j, l2], rb1.at[j, q - 1], s1s.at[q, j], s1r.at[q, j], dev))

    def stage_a(j):
        z = sb1[j, l].astype(F32)
        for q in range(1, nl):
            remote(sb1.at[j, l], rb1.at[j, q - 1], s1s.at[q, j], s1r.at[q, j], loc_dev(q)[1]).wait_recv()
            z = z + rb1[j, q - 1].astype(F32)
        sb2[j] = z.astype(BF16)
        for m in range(1, no):
            o2, dev = lo_dev(m)
            send(remote(sb2.at[j, o2], rb2.at[j, m - 1], s2s.at[m, j], s2r.at[m, j], dev))

    def stage_b(j):
        z = sb2[j, lo].astype(F32)
        for m in range(1, no):
            remote(sb2.at[j, lo], rb2.at[j, m - 1], s2s.at[m, j], s2r.at[m, j], lo_dev(m)[1]).wait_recv()
            z = z + rb2[j, m - 1].astype(F32)
        sb3[j] = z.astype(BF16)
        for k in range(1, nh):
            h2, dev = hi_dev(k)
            send(remote(sb3.at[j, h2], rb3.at[j, k - 1], s3s.at[k, j], s3r.at[k, j], dev))

    def stage_c(j):
        z = sb3[j, hi].astype(F32)
        for k in range(1, nh):
            remote(sb3.at[j, hi], rb3.at[j, k - 1], s3s.at[k, j], s3r.at[k, j], hi_dev(k)[1]).wait_recv()
            z = z + rb3[j, k - 1].astype(F32)
        moe_out[:, j * cw:(j + 1) * cw] = z.astype(BF16)

    for s in range(nc + 7):
        for lag, stage in ((0, stage_m), (2, stage_a), (4, stage_b), (7, stage_c)):
            if 0 <= s - lag < nc:
                stage(s - lag)
    for c in g_sends + out_sends:
        c.wait_send()


def shards(moe_tokens, picked_groups, gate_scores, w_gate, w_up, w_down,
           query_latent, query_rope, cache_latent, cache_rope, cache_lengths):
    ng = lax.axis_size("grp")
    nl = lax.axis_size("loc")
    no = 2 if ng % 2 == 0 else 1
    nh = ng // no
    tk, d = moe_tokens.shape
    reqs, heads, lat = query_latent.shape
    rope, length = cache_rope.shape[1:]
    hl = w_gate.shape[2]
    kc, nc, pc = 4, 7, 4
    cw = d // nc
    rows = ng * nl * tk
    cfg = (ng, nl, no, nh, kc, nc, pc)
    vm = pl.BlockSpec(memory_space=pltpu.VMEM)
    sm = pl.BlockSpec(memory_space=pltpu.SMEM)
    hbm = pl.BlockSpec(memory_space=pl.ANY)
    dma = pltpu.SemaphoreType.DMA
    return tuple(pl.pallas_call(
        functools.partial(fused, cfg),
        out_shape=(jax.ShapeDtypeStruct((tk, d), BF16),
                   jax.ShapeDtypeStruct((reqs, heads, lat), BF16)),
        in_specs=[vm, vm, vm, sm, vm, vm] + [hbm] * 5,
        out_specs=(vm, vm),
        scratch_shapes=[
            pltpu.VMEM((d, hl), BF16), pltpu.VMEM((d, hl), BF16), pltpu.VMEM((hl, d), BF16),
            pltpu.VMEM((reqs, length, lat), BF16), pltpu.VMEM((reqs, rope, length), BF16),
            pltpu.VMEM((heads, length), F32),
            pltpu.VMEM((nl, no, nh, tk, d + EXT), BF16),
            pltpu.VMEM((rows, d + EXT), F32),
            pltpu.VMEM((rows, hl), F32), pltpu.VMEM((rows, hl), F32), pltpu.VMEM((rows, hl), BF16),
            pltpu.VMEM((nc, nl, no, nh, tk, cw), BF16), pltpu.VMEM((nc, nl - 1, no, nh, tk, cw), BF16),
            pltpu.VMEM((nc, no, nh, tk, cw), BF16), pltpu.VMEM((nc, no - 1, nh, tk, cw), BF16),
            pltpu.VMEM((nc, nh, tk, cw), BF16), pltpu.VMEM((nc, nh - 1, tk, cw), BF16),
            dma((2 * kc,)), dma((nc,)), dma((2 * reqs,)),
            dma((nh,)), dma((nh,)), dma((no, nh)), dma((no, nh)), dma((nl, no)), dma((nl, no)),
            dma((nl, nc)), dma((nl, nc)), dma((no, nc)), dma((no, nc)), dma((nh, nc)), dma((nh, nc)),
        ],
        compiler_params=pltpu.CompilerParams(
            collective_id=0, has_side_effects=True, vmem_limit_bytes=63 * 1024 * 1024),
    )(moe_tokens, picked_groups, gate_scores, cache_lengths, query_latent,
      query_rope.reshape(reqs, heads, rope), w_gate, w_up, w_down, cache_latent, cache_rope))


def solution(mesh):
    tokens = P(("rep", "grp", "loc"), None)
    requests = P(("rep", "grp", "loc"), None, None)
    placed = (
        tokens, tokens, tokens,
        P("grp", None, "loc"), P("grp", None, "loc"), P("grp", "loc", None),
        requests, tokens, requests, requests, P(("rep", "grp", "loc")),
    )
    return jax.shard_map(shards, mesh=mesh, in_specs=placed, out_specs=(tokens, requests),
                         check_vma=False)
```

```python
import functools
import jax
import jax.numpy as jnp
from jax import lax
from jax.experimental import pallas as pl
from jax.experimental.pallas import tpu as pltpu
from jax.sharding import PartitionSpec as P

softmax_scale = 192.0 ** (-0.5)
mask_fill = -1e30
MESH = pl.DeviceIdType.MESH
EXT = 128
F32 = jnp.float32
BF16 = jnp.bfloat16


def fused(cfg, *refs):
    ng, nl, no, nh, kc, nc, pc = cfg
    (tok, picks, gsc, lens, qlat, qrope, wg_h, wu_h, wd_h, cl_h, cr_h,
     moe_out, attn_out,
     wg, wu, wd, cl, cr, sc, gat, x32, accg, accu, hs,
     sb1, rb1, sb2, rb2, sb3, rb3,
     wsem, dsem, csem, ghs, ghr, gos, gor, gls, glr,
     s1s, s1r, s2s, s2r, s3s, s3r) = refs
    tk, d = tok.shape
    hl = wg.shape[1]
    reqs, heads, lat = qlat.shape
    length = cl.shape[1]
    g = lax.axis_index("grp")
    l = lax.axis_index("loc")
    hi = g // no
    lo = g % no
    kstep = d // kc
    cw = d // nc

    cache_copies = []
    for r in range(reqs):
        pair = [pltpu.make_async_copy(cl_h.at[r], cl.at[r], csem.at[2 * r]),
                pltpu.make_async_copy(cr_h.at[r], cr.at[r], csem.at[2 * r + 1])]
        for c in pair:
            c.start()
        cache_copies.append(pair)
    w_copies = []
    for k in range(kc):
        rows = pl.ds(k * kstep, kstep)
        pair = [pltpu.make_async_copy(wg_h.at[0, rows], wg.at[rows], wsem.at[2 * k]),
                pltpu.make_async_copy(wu_h.at[0, rows], wu.at[rows], wsem.at[2 * k + 1])]
        w_copies.append(pair)
    d_copies = []
    for j in range(nc):
        cols = pl.ds(j * cw, cw)
        c = pltpu.make_async_copy(wd_h.at[0, :, cols], wd.at[:, cols], dsem.at[j])
        d_copies.append(c)

    def hi_dev(k):
        h2 = lax.rem(hi + k, nh)
        return h2, {"grp": h2 * no + lo, "loc": l}

    def lo_dev(k):
        o2 = lax.rem(lo + k, no)
        return o2, {"grp": hi * no + o2, "loc": l}

    def loc_dev(k):
        l2 = lax.rem(l + k, nl)
        return l2, {"grp": g, "loc": l2}

    lane = lax.broadcasted_iota(jnp.int32, (tk, EXT), 1)
    lane_g = lax.rem(lane, ng)
    weight = jnp.zeros((tk, EXT), F32)
    for k in range(picks.shape[1]):
        weight = weight + jnp.where(picks[:, k:k + 1] == lane_g, gsc[:, k:k + 1], 0.0)
    w1 = weight.astype(BF16).astype(F32)
    w2 = (weight - w1).astype(BF16).astype(F32)
    w3 = weight - w1 - w2
    terms = jnp.where(lane < ng, w1, jnp.where(lane < 2 * ng, w2, jnp.where(lane < 3 * ng, w3, 0.0)))
    gat[l, lo, hi, :, 0:d] = tok[...]
    gat[l, lo, hi, :, d:d + EXT] = terms.astype(BF16)

    barrier = pltpu.get_barrier_semaphore()
    peers = [hi_dev(k)[1] for k in range(1, nh)] + [lo_dev(k)[1] for k in range(1, no)] + [
        loc_dev(k)[1] for k in range(1, nl)]
    for dev in peers:
        pl.semaphore_signal(barrier, inc=1, device_id=dev, device_id_type=MESH)
    pl.semaphore_wait(barrier, len(peers))

    def remote(src, dst, ss, rs, dev):
        return pltpu.make_async_remote_copy(
            src_ref=src, dst_ref=dst, send_sem=ss, recv_sem=rs, device_id=dev, device_id_type=MESH)

    g_sends = []

    def go(copy):
        copy.start()
        g_sends.append(copy)

    mine = gat.at[l, lo, hi]
    for k in range(1, nh):
        go(remote(mine, mine, ghs.at[k], ghr.at[k], hi_dev(k)[1]))

    def forward(k):
        h2 = lax.rem(hi - k + nh, nh)
        blk = gat.at[l, lo, h2]
        if k > 0:
            remote(blk, blk, ghs.at[k], ghr.at[k], hi_dev(k)[1]).wait_recv()
        for m in range(1, no):
            go(remote(blk, blk, gos.at[m, k], gor.at[m, k], lo_dev(m)[1]))

    def loc_send(m):
        o2 = lax.rem(lo - m + no, no)
        if m > 0:
            for k in range(nh):
                blk = gat.at[l, o2, lax.rem(hi - k + nh, nh)]
                remote(blk, blk, gos.at[m, k], gor.at[m, k], lo_dev(m)[1]).wait_recv()
        part = gat.at[l, o2]
        for q in range(1, nl):
            go(remote(part, part, gls.at[q, m], glr.at[q, m], loc_dev(q)[1]))

    def loc_wait(m):
        o2 = lax.rem(lo - m + no, no)
        for q in range(1, nl):
            part = gat.at[lax.rem(l - q + nl, nl), o2]
            remote(part, part, gls.at[q, m], glr.at[q, m], loc_dev(q)[1]).wait_recv()

    forward(0)
    for pair in w_copies:
        for c in pair:
            c.start()
    for c in d_copies:
        c.start()

    pw = length // pc

    def scores_of(r, blocks, top):
        q = qlat[r]
        qr = qrope[r]
        for b in blocks:
            s = lax.dot_general(q, cl[r, b * pw:(b + 1) * pw, :], (((1,), (1,)), ((), ())),
                                preferred_element_type=F32)
            s = s + jnp.dot(qr, cr[r, :, b * pw:(b + 1) * pw], preferred_element_type=F32)
            pos = lax.broadcasted_iota(jnp.int32, (heads, pw), 1) + b * pw
            s = jnp.where(pos < lens[r], s * softmax_scale, mask_fill)
            sc[:, b * pw:(b + 1) * pw] = s
            t = jnp.max(s, axis=1, keepdims=True)
            top = t if top is None else jnp.maximum(top, t)
        return top

    def values_of(r, blocks, top, acc, total):
        for b in blocks:
            p = jnp.exp(sc[:, b * pw:(b + 1) * pw] - top)
            total = total + jnp.sum(p, axis=1, keepdims=True)
            acc = acc + jnp.dot(p.astype(BF16), cl[r, b * pw:(b + 1) * pw, :],
                                preferred_element_type=F32)
        return acc, total

    steps = [functools.partial(forward, k) for k in range(1, nh)]
    steps.append(functools.partial(loc_send, 0))
    half = pc // 2
    halves = (range(0, half), range(half, pc))

    def step():
        if steps:
            steps.pop(0)()

    for r in range(reqs):
        for c in cache_copies[r]:
            c.wait()
        top = scores_of(r, halves[0], None)
        step()
        top = scores_of(r, halves[1], top)
        step()
        acc, total = values_of(r, halves[0], top, jnp.zeros((heads, lat), F32), jnp.zeros((heads, 1), F32))
        step()
        if r == reqs - 1:
            while steps:
                step()
            for m in range(1, no):
                loc_send(m)
        acc, total = values_of(r, halves[1], top, acc, total)
        step()
        attn_out[r] = (acc / total).astype(BF16)
    while steps:
        step()
    for m in range(no):
        loc_wait(m)

    per = no * nh

    pack = max(1, 8 // tk)

    def put(i, _):
        parts = []
        for u in range(pack):
            at = i * pack + u
            rest = at % per
            parts.append(gat[at // per, rest // nh, rest % nh].astype(F32))
        x32[pl.ds(pl.multiple_of(i * (pack * tk), 8), pack * tk), :] = jnp.concatenate(parts, axis=0)
        return 0

    packs = nl * per // pack
    lax.fori_loop(0, packs, put, 0, unroll=min(8, packs))

    nt = min(256, hl)
    for k in range(kc):
        for c in w_copies[k]:
            c.wait()
        xk = x32[:, k * kstep:(k + 1) * kstep].astype(BF16)
        for n in range(hl // nt):
            cols = slice(n * nt, (n + 1) * nt)
            rows = slice(k * kstep, (k + 1) * kstep)
            pg = jnp.dot(xk, wg[rows, cols], preferred_element_type=F32)
            pu = jnp.dot(xk, wu[rows, cols], preferred_element_type=F32)
            if k > 0:
                pg = accg[:, cols] + pg
                pu = accu[:, cols] + pu
            if k < kc - 1:
                accg[:, cols] = pg
                accu[:, cols] = pu
            else:
                hs[:, cols] = (pg / (1.0 + jnp.exp(-pg)) * pu).astype(BF16)

    wlane = lax.broadcasted_iota(jnp.int32, (x32.shape[0], EXT), 1)
    hit = (lax.rem(wlane, ng) == g) & (wlane < 3 * ng)
    wcol = jnp.sum(jnp.where(hit, x32[:, d:d + EXT], 0.0), axis=1, keepdims=True)

    out_sends = []

    def send(copy):
        copy.start()
        out_sends.append(copy)

    def stage_m(j):
        d_copies[j].wait()
        y = jnp.dot(hs[...], wd[:, j * cw:(j + 1) * cw], preferred_element_type=F32) * wcol
        for i in range(nl * per):
            rest = i % per
            sb1[j, i // per, rest // nh, rest % nh] = y[i * tk:(i + 1) * tk].astype(BF16)
        for q in range(1, nl):
            l2, dev = loc_dev(q)
            send(remote(sb1.at[j, l2], rb1.at[j, q - 1], s1s.at[q, j], s1r.at[q, j], dev))

    def stage_a(j):
        z = sb1[j, l].astype(F32)
        for q in range(1, nl):
            remote(sb1.at[j, l], rb1.at[j, q - 1], s1s.at[q, j], s1r.at[q, j], loc_dev(q)[1]).wait_recv()
            z = z + rb1[j, q - 1].astype(F32)
        sb2[j] = z.astype(BF16)
        for m in range(1, no):
            o2, dev = lo_dev(m)
            send(remote(sb2.at[j, o2], rb2.at[j, m - 1], s2s.at[m, j], s2r.at[m, j], dev))

    def stage_b(j):
        z = sb2[j, lo].astype(F32)
        for m in range(1, no):
            remote(sb2.at[j, lo], rb2.at[j, m - 1], s2s.at[m, j], s2r.at[m, j], lo_dev(m)[1]).wait_recv()
            z = z + rb2[j, m - 1].astype(F32)
        sb3[j] = z.astype(BF16)
        for k in range(1, nh):
            h2, dev = hi_dev(k)
            send(remote(sb3.at[j, h2], rb3.at[j, k - 1], s3s.at[k, j], s3r.at[k, j], dev))

    def stage_c(j):
        z = sb3[j, hi].astype(F32)
        for k in range(1, nh):
            remote(sb3.at[j, hi], rb3.at[j, k - 1], s3s.at[k, j], s3r.at[k, j], hi_dev(k)[1]).wait_recv()
            z = z + rb3[j, k - 1].astype(F32)
        moe_out[:, j * cw:(j + 1) * cw] = z.astype(BF16)

    for s in range(nc + 7):
        for lag, stage in ((0, stage_m), (2, stage_a), (4, stage_b), (7, stage_c)):
            if 0 <= s - lag < nc:
                stage(s - lag)
    for c in g_sends + out_sends:
        c.wait_send()


def shards(moe_tokens, picked_groups, gate_scores, w_gate, w_up, w_down,
           query_latent, query_rope, cache_latent, cache_rope, cache_lengths):
    ng = lax.axis_size("grp")
    nl = lax.axis_size("loc")
    no = 2 if ng % 2 == 0 else 1
    nh = ng // no
    tk, d = moe_tokens.shape
    reqs, heads, lat = query_latent.shape
    rope, length = cache_rope.shape[1:]
    hl = w_gate.shape[2]
    kc, nc, pc = 4, 7, 4
    cw = d // nc
    rows = ng * nl * tk
    cfg = (ng, nl, no, nh, kc, nc, pc)
    vm = pl.BlockSpec(memory_space=pltpu.VMEM)
    sm = pl.BlockSpec(memory_space=pltpu.SMEM)
    hbm = pl.BlockSpec(memory_space=pl.ANY)
    dma = pltpu.SemaphoreType.DMA
    return tuple(pl.pallas_call(
        functools.partial(fused, cfg),
        out_shape=(jax.ShapeDtypeStruct((tk, d), BF16),
                   jax.ShapeDtypeStruct((reqs, heads, lat), BF16)),
        in_specs=[vm, vm, vm, sm, vm, vm] + [hbm] * 5,
        out_specs=(vm, vm),
        scratch_shapes=[
            pltpu.VMEM((d, hl), BF16), pltpu.VMEM((d, hl), BF16), pltpu.VMEM((hl, d), BF16),
            pltpu.VMEM((reqs, length, lat), BF16), pltpu.VMEM((reqs, rope, length), BF16),
            pltpu.VMEM((heads, length), F32),
            pltpu.VMEM((nl, no, nh, tk, d + EXT), BF16),
            pltpu.VMEM((rows, d + EXT), F32),
            pltpu.VMEM((rows, hl), F32), pltpu.VMEM((rows, hl), F32), pltpu.VMEM((rows, hl), BF16),
            pltpu.VMEM((nc, nl, no, nh, tk, cw), BF16), pltpu.VMEM((nc, nl - 1, no, nh, tk, cw), BF16),
            pltpu.VMEM((nc, no, nh, tk, cw), BF16), pltpu.VMEM((nc, no - 1, nh, tk, cw), BF16),
            pltpu.VMEM((nc, nh, tk, cw), BF16), pltpu.VMEM((nc, nh - 1, tk, cw), BF16),
            dma((2 * kc,)), dma((nc,)), dma((2 * reqs,)),
            dma((nh,)), dma((nh,)), dma((no, nh)), dma((no, nh)), dma((nl, no)), dma((nl, no)),
            dma((nl, nc)), dma((nl, nc)), dma((no, nc)), dma((no, nc)), dma((nh, nc)), dma((nh, nc)),
        ],
        compiler_params=pltpu.CompilerParams(
            collective_id=0, has_side_effects=True, vmem_limit_bytes=63 * 1024 * 1024),
    )(moe_tokens, picked_groups, gate_scores, cache_lengths, query_latent,
      query_rope.reshape(reqs, heads, rope), w_gate, w_up, w_down, cache_latent, cache_rope))


def solution(mesh):
    tokens = P(("rep", "grp", "loc"), None)
    requests = P(("rep", "grp", "loc"), None, None)
    placed = (
        tokens, tokens, tokens,
        P("grp", None, "loc"), P("grp", None, "loc"), P("grp", "loc", None),
        requests, tokens, requests, requests, P(("rep", "grp", "loc")),
    )
    return jax.shard_map(shards, mesh=mesh, in_specs=placed, out_specs=(tokens, requests),
                         check_vma=False)
```

```python
import functools
import jax
import jax.numpy as jnp
from jax import lax
from jax.experimental import pallas as pl
from jax.experimental.pallas import tpu as pltpu
from jax.sharding import PartitionSpec as P

softmax_scale = 192.0 ** (-0.5)
mask_fill = -1e30
MESH = pl.DeviceIdType.MESH
EXT = 128
F32 = jnp.float32
BF16 = jnp.bfloat16


def fused(cfg, *refs):
    ng, nl, no, nh, kc, nc, pc = cfg
    (tok, picks, gsc, lens, qlat, qrope, wg_h, wu_h, wd_h, cl_h, cr_h,
     moe_out, attn_out,
     wg, wu, wd, cl, cr, sc, gat, x32, accg, accu, hs,
     sb1, rb1, sb2, rb2, sb3, rb3,
     wsem, dsem, csem, ghs, ghr, gos, gor, gls, glr,
     s1s, s1r, s2s, s2r, s3s, s3r) = refs
    tk, d = tok.shape
    hl = wg.shape[1]
    reqs, heads, lat = qlat.shape
    length = cl.shape[1]
    g = lax.axis_index("grp")
    l = lax.axis_index("loc")
    hi = g // no
    lo = g % no
    kstep = d // kc
    cw = d // nc

    cache_copies = []
    for r in range(reqs):
        pair = [pltpu.make_async_copy(cl_h.at[r], cl.at[r], csem.at[2 * r]),
                pltpu.make_async_copy(cr_h.at[r], cr.at[r], csem.at[2 * r + 1])]
        for c in pair:
            c.start()
        cache_copies.append(pair)
    w_copies = []
    for k in range(kc):
        rows = pl.ds(k * kstep, kstep)
        pair = [pltpu.make_async_copy(wg_h.at[0, rows], wg.at[rows], wsem.at[2 * k]),
                pltpu.make_async_copy(wu_h.at[0, rows], wu.at[rows], wsem.at[2 * k + 1])]
        w_copies.append(pair)
    d_copies = []
    for j in range(nc):
        cols = pl.ds(j * cw, cw)
        c = pltpu.make_async_copy(wd_h.at[0, :, cols], wd.at[:, cols], dsem.at[j])
        d_copies.append(c)

    def hi_dev(k):
        h2 = lax.rem(hi + k, nh)
        return h2, {"grp": h2 * no + lo, "loc": l}

    def lo_dev(k):
        o2 = lax.rem(lo + k, no)
        return o2, {"grp": hi * no + o2, "loc": l}

    def loc_dev(k):
        l2 = lax.rem(l + k, nl)
        return l2, {"grp": g, "loc": l2}

    lane = lax.broadcasted_iota(jnp.int32, (tk, EXT), 1)
    lane_g = lax.rem(lane, ng)
    weight = jnp.zeros((tk, EXT), F32)
    for k in range(picks.shape[1]):
        weight = weight + jnp.where(picks[:, k:k + 1] == lane_g, gsc[:, k:k + 1], 0.0)
    w1 = weight.astype(BF16).astype(F32)
    w2 = (weight - w1).astype(BF16).astype(F32)
    w3 = weight - w1 - w2
    terms = jnp.where(lane < ng, w1, jnp.where(lane < 2 * ng, w2, jnp.where(lane < 3 * ng, w3, 0.0)))
    gat[l, lo, hi, :, 0:d] = tok[...]
    gat[l, lo, hi, :, d:d + EXT] = terms.astype(BF16)

    barrier = pltpu.get_barrier_semaphore()
    peers = [hi_dev(k)[1] for k in range(1, nh)] + [lo_dev(k)[1] for k in range(1, no)] + [
        loc_dev(k)[1] for k in range(1, nl)]
    for dev in peers:
        pl.semaphore_signal(barrier, inc=1, device_id=dev, device_id_type=MESH)
    pl.semaphore_wait(barrier, len(peers))

    def remote(src, dst, ss, rs, dev):
        return pltpu.make_async_remote_copy(
            src_ref=src, dst_ref=dst, send_sem=ss, recv_sem=rs, device_id=dev, device_id_type=MESH)

    g_sends = []

    def go(copy):
        copy.start()
        g_sends.append(copy)

    mine = gat.at[l, lo, hi]
    for k in range(1, nh):
        go(remote(mine, mine, ghs.at[k], ghr.at[k], hi_dev(k)[1]))

    def forward(k):
        h2 = lax.rem(hi - k + nh, nh)
        blk = gat.at[l, lo, h2]
        if k > 0:
            remote(blk, blk, ghs.at[k], ghr.at[k], hi_dev(k)[1]).wait_recv()
        for m in range(1, no):
            go(remote(blk, blk, gos.at[m, k], gor.at[m, k], lo_dev(m)[1]))

    def loc_send(m):
        o2 = lax.rem(lo - m + no, no)
        if m > 0:
            for k in range(nh):
                blk = gat.at[l, o2, lax.rem(hi - k + nh, nh)]
                remote(blk, blk, gos.at[m, k], gor.at[m, k], lo_dev(m)[1]).wait_recv()
        part = gat.at[l, o2]
        for q in range(1, nl):
            go(remote(part, part, gls.at[q, m], glr.at[q, m], loc_dev(q)[1]))

    def loc_wait(m):
        o2 = lax.rem(lo - m + no, no)
        for q in range(1, nl):
            part = gat.at[lax.rem(l - q + nl, nl), o2]
            remote(part, part, gls.at[q, m], glr.at[q, m], loc_dev(q)[1]).wait_recv()

    forward(0)
    for pair in w_copies:
        for c in pair:
            c.start()

    pw = length // pc

    def scores_of(r, blocks, top):
        q = qlat[r]
        qr = qrope[r]
        for b in blocks:
            s = lax.dot_general(q, cl[r, b * pw:(b + 1) * pw, :], (((1,), (1,)), ((), ())),
                                preferred_element_type=F32)
            s = s + jnp.dot(qr, cr[r, :, b * pw:(b + 1) * pw], preferred_element_type=F32)
            pos = lax.broadcasted_iota(jnp.int32, (heads, pw), 1) + b * pw
            s = jnp.where(pos < lens[r], s * softmax_scale, mask_fill)
            sc[:, b * pw:(b + 1) * pw] = s
            t = jnp.max(s, axis=1, keepdims=True)
            top = t if top is None else jnp.maximum(top, t)
        return top

    def values_of(r, blocks, top, acc, total):
        for b in blocks:
            p = jnp.exp(sc[:, b * pw:(b + 1) * pw] - top)
            total = total + jnp.sum(p, axis=1, keepdims=True)
            acc = acc + jnp.dot(p.astype(BF16), cl[r, b * pw:(b + 1) * pw, :],
                                preferred_element_type=F32)
        return acc, total

    steps = [functools.partial(forward, k) for k in range(1, nh)]
    steps.append(functools.partial(loc_send, 0))
    half = pc // 2
    halves = (range(0, half), range(half, pc))

    def step():
        if steps:
            steps.pop(0)()

    for r in range(reqs):
        for c in cache_copies[r]:
            c.wait()
        if r == reqs - 1:
            for c in d_copies:
                c.start()
        top = scores_of(r, halves[0], None)
        step()
        top = scores_of(r, halves[1], top)
        step()
        acc, total = values_of(r, halves[0], top, jnp.zeros((heads, lat), F32), jnp.zeros((heads, 1), F32))
        step()
        if r == reqs - 1:
            while steps:
                step()
            for m in range(1, no):
                loc_send(m)
        acc, total = values_of(r, halves[1], top, acc, total)
        step()
        attn_out[r] = (acc / total).astype(BF16)
    while steps:
        step()
    for m in range(no):
        loc_wait(m)

    per = no * nh

    pack = max(1, 8 // tk)

    def put(i, _):
        parts = []
        for u in range(pack):
            at = i * pack + u
            rest = at % per
            parts.append(gat[at // per, rest // nh, rest % nh].astype(F32))
        x32[pl.ds(pl.multiple_of(i * (pack * tk), 8), pack * tk), :] = jnp.concatenate(parts, axis=0)
        return 0

    packs = nl * per // pack
    lax.fori_loop(0, packs, put, 0, unroll=min(8, packs))

    nt = min(256, hl)
    for k in range(kc):
        for c in w_copies[k]:
            c.wait()
        xk = x32[:, k * kstep:(k + 1) * kstep].astype(BF16)
        for n in range(hl // nt):
            cols = slice(n * nt, (n + 1) * nt)
            rows = slice(k * kstep, (k + 1) * kstep)
            pg = jnp.dot(xk, wg[rows, cols], preferred_element_type=F32)
            pu = jnp.dot(xk, wu[rows, cols], preferred_element_type=F32)
            if k > 0:
                pg = accg[:, cols] + pg
                pu = accu[:, cols] + pu
            if k < kc - 1:
                accg[:, cols] = pg
                accu[:, cols] = pu
            else:
                hs[:, cols] = (pg / (1.0 + jnp.exp(-pg)) * pu).astype(BF16)

    wlane = lax.broadcasted_iota(jnp.int32, (x32.shape[0], EXT), 1)
    hit = (lax.rem(wlane, ng) == g) & (wlane < 3 * ng)
    wcol = jnp.sum(jnp.where(hit, x32[:, d:d + EXT], 0.0), axis=1, keepdims=True)

    out_sends = []

    def send(copy):
        copy.start()
        out_sends.append(copy)

    def stage_m(j):
        d_copies[j].wait()
        y = jnp.dot(hs[...], wd[:, j * cw:(j + 1) * cw], preferred_element_type=F32) * wcol
        for i in range(nl * per):
            rest = i % per
            sb1[j, i // per, rest // nh, rest % nh] = y[i * tk:(i + 1) * tk].astype(BF16)
        for q in range(1, nl):
            l2, dev = loc_dev(q)
            send(remote(sb1.at[j, l2], rb1.at[j, q - 1], s1s.at[q, j], s1r.at[q, j], dev))

    def stage_a(j):
        z = sb1[j, l].astype(F32)
        for q in range(1, nl):
            remote(sb1.at[j, l], rb1.at[j, q - 1], s1s.at[q, j], s1r.at[q, j], loc_dev(q)[1]).wait_recv()
            z = z + rb1[j, q - 1].astype(F32)
        sb2[j] = z.astype(BF16)
        for m in range(1, no):
            o2, dev = lo_dev(m)
            send(remote(sb2.at[j, o2], rb2.at[j, m - 1], s2s.at[m, j], s2r.at[m, j], dev))

    def stage_b(j):
        z = sb2[j, lo].astype(F32)
        for m in range(1, no):
            remote(sb2.at[j, lo], rb2.at[j, m - 1], s2s.at[m, j], s2r.at[m, j], lo_dev(m)[1]).wait_recv()
            z = z + rb2[j, m - 1].astype(F32)
        sb3[j] = z.astype(BF16)
        for k in range(1, nh):
            h2, dev = hi_dev(k)
            send(remote(sb3.at[j, h2], rb3.at[j, k - 1], s3s.at[k, j], s3r.at[k, j], dev))

    def stage_c(j):
        z = sb3[j, hi].astype(F32)
        for k in range(1, nh):
            remote(sb3.at[j, hi], rb3.at[j, k - 1], s3s.at[k, j], s3r.at[k, j], hi_dev(k)[1]).wait_recv()
            z = z + rb3[j, k - 1].astype(F32)
        moe_out[:, j * cw:(j + 1) * cw] = z.astype(BF16)

    for s in range(nc + 6):
        for lag, stage in ((0, stage_m), (1, stage_a), (3, stage_b), (6, stage_c)):
            if 0 <= s - lag < nc:
                stage(s - lag)
    for c in g_sends + out_sends:
        c.wait_send()


def shards(moe_tokens, picked_groups, gate_scores, w_gate, w_up, w_down,
           query_latent, query_rope, cache_latent, cache_rope, cache_lengths):
    ng = lax.axis_size("grp")
    nl = lax.axis_size("loc")
    no = 2 if ng % 2 == 0 else 1
    nh = ng // no
    tk, d = moe_tokens.shape
    reqs, heads, lat = query_latent.shape
    rope, length = cache_rope.shape[1:]
    hl = w_gate.shape[2]
    kc, nc, pc = 4, 7, 4
    cw = d // nc
    rows = ng * nl * tk
    cfg = (ng, nl, no, nh, kc, nc, pc)
    vm = pl.BlockSpec(memory_space=pltpu.VMEM)
    sm = pl.BlockSpec(memory_space=pltpu.SMEM)
    hbm = pl.BlockSpec(memory_space=pl.ANY)
    dma = pltpu.SemaphoreType.DMA
    return tuple(pl.pallas_call(
        functools.partial(fused, cfg),
        out_shape=(jax.ShapeDtypeStruct((tk, d), BF16),
                   jax.ShapeDtypeStruct((reqs, heads, lat), BF16)),
        in_specs=[vm, vm, vm, sm, vm, vm] + [hbm] * 5,
        out_specs=(vm, vm),
        scratch_shapes=[
            pltpu.VMEM((d, hl), BF16), pltpu.VMEM((d, hl), BF16), pltpu.VMEM((hl, d), BF16),
            pltpu.VMEM((reqs, length, lat), BF16), pltpu.VMEM((reqs, rope, length), BF16),
            pltpu.VMEM((heads, length), F32),
            pltpu.VMEM((nl, no, nh, tk, d + EXT), BF16),
            pltpu.VMEM((rows, d + EXT), F32),
            pltpu.VMEM((rows, hl), F32), pltpu.VMEM((rows, hl), F32), pltpu.VMEM((rows, hl), BF16),
            pltpu.VMEM((nc, nl, no, nh, tk, cw), BF16), pltpu.VMEM((nc, nl - 1, no, nh, tk, cw), BF16),
            pltpu.VMEM((nc, no, nh, tk, cw), BF16), pltpu.VMEM((nc, no - 1, nh, tk, cw), BF16),
            pltpu.VMEM((nc, nh, tk, cw), BF16), pltpu.VMEM((nc, nh - 1, tk, cw), BF16),
            dma((2 * kc,)), dma((nc,)), dma((2 * reqs,)),
            dma((nh,)), dma((nh,)), dma((no, nh)), dma((no, nh)), dma((nl, no)), dma((nl, no)),
            dma((nl, nc)), dma((nl, nc)), dma((no, nc)), dma((no, nc)), dma((nh, nc)), dma((nh, nc)),
        ],
        compiler_params=pltpu.CompilerParams(
            collective_id=0, has_side_effects=True, vmem_limit_bytes=63 * 1024 * 1024),
    )(moe_tokens, picked_groups, gate_scores, cache_lengths, query_latent,
      query_rope.reshape(reqs, heads, rope), w_gate, w_up, w_down, cache_latent, cache_rope))


def solution(mesh):
    tokens = P(("rep", "grp", "loc"), None)
    requests = P(("rep", "grp", "loc"), None, None)
    placed = (
        tokens, tokens, tokens,
        P("grp", None, "loc"), P("grp", None, "loc"), P("grp", "loc", None),
        requests, tokens, requests, requests, P(("rep", "grp", "loc")),
    )
    return jax.shard_map(shards, mesh=mesh, in_specs=placed, out_specs=(tokens, requests),
                         check_vma=False)
```
